32 devices in a mesh: dp: 8 (over z, y), mp: 4 (over x, core).
Axes of the slice: x: 2, y: 2, z: 4, core: 2. Of those that a mesh axis runs over, the one named last changes fastest.
Arguments:
- query_hidden: bfloat16 [256, 32, 768], P('dp', None, 'mp'), may hold values from -6 to 6
- query_proj: bfloat16 [768, 128], P('mp'), may hold values from -0.21875 to 0.21875
- passages: bfloat16 [512, 128, 128], P(('dp', 'mp')), may hold values from -6 to 6
- teacher: float32 [256, 4, 64], P('dp'), may hold values from -8 to 8
- neg_blocks: int32 [256, 4], P('dp'), may hold values from 0 to 7, all different within a row; in each aligned block of 32 rows (0 to 31, 32 to 63, ...) at most 16 rows name the same one
Outputs:
- kl_loss: float32 [256], P('dp')
The draws below stay inside these ranges and needn't reach their ends.
Inputs may be any that keep to these rules, and one draw needn't show every extreme that they name: `neg_blocks`: each query names 4 different blocks. Among the 32 queries of one dp index no block is named more than 16 times, and some block is named exactly 16 times.
All inputs are finite; a program needn't handle non-finite values.
Results may differ from the reference program's by a relative error of at most 0.0003.
Values may be sent and summed in bfloat16 or wider, within the bound.
A program may use at most 64 MiB of HBM per device.

```python
import math
import jax
import jax.numpy as jnp
import numpy as np
from jax import lax

H = 768
E = 128
QT = 32
PT = 128
BP = 64
NB = 4
QD = 32
QUERIES = 256
BLOCKS = 8
PASSAGES = 512
CAP = 16


def level_of(own_key, extent, pieces, least, top_value):
    def one(dim, shards_of):
        draws = jax.random.uniform(jax.random.fold_in(jax.random.fold_in(own_key, 6), dim), (shards_of,), jnp.float32, least / len(pieces), top_value / len(pieces))
        return jnp.repeat(jnp.exp(draws), extent[dim] // shards_of).reshape((-1,) + (1,) * (len(extent) - dim - 1))

    factor_of = one(*pieces[0])
    for cut in pieces[1:]:
        factor_of = factor_of * one(*cut)
    return factor_of


def deal_out(stream_key, own, number, rows, amount, top, reach, lean):
    order = jax.random.permutation(stream_key, amount)
    heavy_load, ordinary = load_shares(amount, rows * top, reach, lean, True), load_shares(amount, rows * top, reach, lean, False)
    places = jnp.arange(amount)

    def named(lengths, offset_by):
        used = int((lengths > 0).sum())
        fixed = max(1, used // 4)
        passed = fixed + (places - fixed + offset_by * (used - fixed)) % max(1, amount - fixed)
        return jnp.zeros((amount,), jnp.int32).at[order[jnp.where(places < fixed, places, passed)]].set(jnp.asarray(lengths, jnp.int32))

    lengths = jnp.where(number % 4 == 0, named(heavy_load, number // 4), named(ordinary, number - number // 4 - 1))
    mixed = jax.random.permutation(jax.random.fold_in(own, 3), amount)
    donor, receiver = mixed[0:amount // 2 * 2:2], mixed[1:amount // 2 * 2:2]
    room = jnp.minimum(lengths[donor] - 1, reach - lengths[receiver]) // 2
    room = jnp.where((donor == order[0]) | (receiver == order[0]) | (lengths[receiver] == 0), 0, jnp.maximum(room, 0))
    passed = jax.random.randint(jax.random.fold_in(own, 4), (amount // 2,), 0, 1 << 20) % (room + 1)
    lengths = lengths.at[donor].add(-passed).at[receiver].add(passed)
    members = jnp.searchsorted(jnp.cumsum(lengths), jnp.arange(rows * top), side="right").astype(jnp.int32)
    grid = members.reshape(top, rows).T
    grid = grid[jax.random.permutation(jax.random.fold_in(own, 1), rows)]
    offset_by = jax.random.randint(jax.random.fold_in(own, 2), (rows, 1), 0, top)
    return jnp.take_along_axis(grid, (jnp.arange(top)[None, :] + offset_by) % top, axis=1)


def load_shares(number_of, total, most, slope, full):
    weights = [(1 << 20) // math.isqrt(rank ** slope) + 1 for rank in range(1, number_of + 1)]
    largest = most if full else min(most, max(-(-total // number_of), total * weights[0] // sum(weights)))
    least = 1 if total - largest >= number_of - 1 else 0
    given, surplus = [largest] + [least] * (number_of - 1), total - largest - least * (number_of - 1)
    while surplus > 0:
        candidates = [i for i in range(1, number_of) if given[i] < largest] or [i for i in range(1, number_of) if given[i] < most]
        mass, remaining = sum([weights[i] for i in candidates]), surplus
        for i in candidates:
            more = min(most - given[i], max(1, remaining * weights[i] // mass), surplus)
            given[i] = given[i] + more
            surplus = surplus - more
    return np.array(given)


def gaussian(stream_key, dims, deviation, bound, pieces=(), dtype=jnp.bfloat16):
    result = jax.random.normal(stream_key, dims, jnp.float32) * deviation
    if len(pieces) > 0:
        result = level_of(stream_key, dims, pieces, -0.22, 0.18) * result
    return jnp.clip(result, min=-bound, max=bound).astype(dtype)


def setup_inputs(seed: int = 0) -> dict:
    keys = jax.random.split(jax.random.key(seed), 6)
    query_hidden = gaussian(keys[0], (QUERIES, QT, H), 1.0, 6.0, ((0, 8), (2, 4)))
    query_proj = gaussian(keys[1], (H, E), H ** -0.5, 0.21875, ((0, 4),))
    passages = gaussian(keys[2], (PASSAGES, PT, E), 1.0, 6.0, ((0, 32),))
    teacher = gaussian(keys[3], (QUERIES, NB, BP), 2.0, 8.0, ((0, 8),), jnp.float32)
    neg_blocks_keys = jax.random.split(jax.random.fold_in(keys[4], 1), QUERIES // QD)
    neg_blocks_turns = jax.random.permutation(jax.random.fold_in(keys[4], 3), QUERIES // QD)
    neg_blocks = jax.vmap(lambda own, number: deal_out(jax.random.fold_in(keys[4], 2), own, number, QD, BLOCKS, NB, CAP, 2))(neg_blocks_keys, neg_blocks_turns).reshape((QUERIES, NB))
    return {"query_hidden": query_hidden, "query_proj": query_proj, "passages": passages, "teacher": teacher, "neg_blocks": neg_blocks}


softness = 0.1

def unit_rows(values):
    return values * lax.rsqrt(lax.optimization_barrier(jnp.sum(values * values, axis=-1, keepdims=True)) + 1e-06)

def reference(query_hidden, query_proj, passages, teacher, neg_blocks):
    projected = jnp.einsum('qth,he->qte', query_hidden.astype(jnp.float32), query_proj.astype(jnp.float32))
    query_vecs = unit_rows(projected).astype(jnp.bfloat16)
    passage_vecs = unit_rows(passages.astype(jnp.float32)).astype(jnp.bfloat16)
    blocks = passage_vecs.reshape(BLOCKS, BP, PT, E)

    def query_scores(query_pair):
        vectors, chosen_ids = query_pair
        chosen = blocks[chosen_ids]
        sims = jnp.einsum('ie,kpje->ikpj', vectors.astype(jnp.float32), chosen.astype(jnp.float32))
        softened = softness * jnp.log(lax.optimization_barrier(jnp.sum(jnp.exp(sims / softness), axis=-1)))
        return lax.optimization_barrier(jnp.sum(softened, axis=0))
    student = lax.map(query_scores, (query_vecs, neg_blocks))
    teacher_logp = teacher - jnp.log(lax.optimization_barrier(jnp.sum(jnp.exp(teacher), axis=(1, 2), keepdims=True)))
    kl_loss = lax.optimization_barrier(jnp.sum(jnp.exp(teacher_logp) * (teacher_logp - student), axis=(1, 2))) + jnp.log(lax.optimization_barrier(jnp.sum(jnp.exp(student), axis=(1, 2))))
    return kl_loss
```

```python
import functools
import jax
import jax.numpy as jnp
from jax import lax
from jax.experimental import pallas as pl
from jax.experimental.pallas import tpu as pltpu
from jax.sharding import PartitionSpec as P

softness = 0.1
log2_e = 1.4426950408889634
group = 8


def unit_rows(values):
    return values * lax.rsqrt(jnp.sum(values * values, axis=-1, keepdims=True) + 1e-06)


def fused_kernel(
    dp, mp, cap,
    hid_ref, proj_ref, pas_ref, teach_ref, slotq_ref, slote_ref,
    out_ref,
    part, send_a, recv_a, pvecs, pick, send_b, queries, sums, send_r, recv_r, lp_perm,
    a_send, a_recv, p_send, p_recv, b_send, b_recv, c_send, c_recv, r_send, r_recv,
):
    d = lax.axis_index("dp")
    m = lax.axis_index("mp")
    x, c = m // 2, m % 2
    qd, qt = hid_ref.shape[0], hid_ref.shape[1]
    emb = proj_ref.shape[1]
    pick_count = teach_ref.shape[1]
    share = qt // mp
    half = cap // 2
    rows_b = half * share
    own_p = pas_ref.shape[0]
    pt = pas_ref.shape[1]
    chip_p = 2 * own_p
    slots = dp * cap

    def remote(src, dst, ssem, rsem, dd, mm):
        return pltpu.make_async_remote_copy(
            src_ref=src, dst_ref=dst, send_sem=ssem, recv_sem=rsem,
            device_id=(dd, mm), device_id_type=pl.DeviceIdType.MESH,
        )

    barrier = pltpu.get_barrier_semaphore()
    for j in range(dp):
        for i in range(mp):
            if j or i:
                pl.semaphore_signal(
                    barrier, inc=1, device_id=((d + j) % dp, (m + i) % mp),
                    device_id_type=pl.DeviceIdType.MESH,
                )

    projected = jnp.dot(
        hid_ref[...].reshape(qd * qt, hid_ref.shape[2]), proj_ref[...],
        preferred_element_type=jnp.float32,
    ).reshape(qd, qt, emb)
    for k in range(mp):
        piece = projected[:, k * share:(k + 1) * share, :].reshape(qd * share, emb)
        part[k] = piece
        send_a[k] = piece.astype(jnp.bfloat16)

    pl.semaphore_wait(barrier, dp * mp - 1)

    copies = []
    for i in range(1, mp):
        to = (m + i) % mp
        cp = remote(send_a.at[to], recv_a.at[m], a_send.at[i], a_recv.at[m], d, to)
        cp.start()
        copies.append(cp)

    pvecs[c] = unit_rows(pas_ref[...].reshape(own_p * pt, emb).astype(jnp.float32)).astype(
        jnp.bfloat16
    )
    cp = remote(pvecs.at[c], pvecs.at[c], p_send, p_recv, d, 2 * x + 1 - c)
    cp.start()
    copies.append(cp)

    row = lax.broadcasted_iota(jnp.int32, (cap * share, qd * share), 0)
    for b in range(dp):
        hit = slote_ref[0:1, :] == row + b * cap * share
        for k in range(1, pick_count):
            hit = hit | (slote_ref[k:k + 1, :] == row + b * cap * share)
        pick[b] = jnp.where(hit, 1.0, 0.0).astype(jnp.bfloat16)

    total = part[m]
    for i in range(1, mp):
        src = (m + i) % mp
        remote(send_a.at[src], recv_a.at[src], a_send.at[i], a_recv.at[src], d, src).wait_recv()
        total = total + recv_a[src].astype(jnp.float32)
    share_vecs = unit_rows(total).astype(jnp.bfloat16)

    for j in range(dp):
        b = (d + j) % dp
        chosen = jnp.dot(pick[b], share_vecs, preferred_element_type=jnp.float32).astype(
            jnp.bfloat16
        )
        send_b[j] = chosen.reshape(2, rows_b, emb)
        for cc in (1, 0):
            to_c = c if cc == 0 else 1 - c
            if j == 0 and cc == 0:
                queries[d, m] = send_b[0, c]
                continue
            cp = remote(
                send_b.at[j, to_c], queries.at[d, m], b_send.at[j, cc], b_recv.at[d, c],
                b, 2 * x + to_c,
            )
            cp.start()
            copies.append(cp)

    slot_row = lax.broadcasted_iota(jnp.int32, (slots, qd), 0)
    norm = jnp.zeros((qd, 1), jnp.float32)
    for k in range(pick_count):
        norm = norm + jnp.sum(jnp.exp(teach_ref[:, k, :]), axis=-1, keepdims=True)
    log_norm = jnp.log(norm)
    perm = jnp.zeros((slots, teach_ref.shape[2]), jnp.float32)
    for k in range(pick_count):
        place = jnp.where(slotq_ref[k:k + 1, :] == slot_row, 1.0, 0.0)
        perm = perm + jnp.dot(
            place, teach_ref[:, k, :] - log_norm, precision=lax.Precision.HIGHEST,
            preferred_element_type=jnp.float32,
        )
    lp_perm[...] = perm

    lane = lax.broadcasted_iota(jnp.int32, (half, mp * rows_b), 1)
    slot_of = lax.broadcasted_iota(jnp.int32, (half, mp * rows_b), 0)
    fold = jnp.where((lane // share) % half == slot_of, 1.0, 0.0)

    def arrive(j):
        src_d = (d - j + dp) % dp
        for cc in (1, 0):
            if j == 0 and cc == 0:
                continue
            src_c = c if cc == 0 else 1 - c
            remote(
                send_b.at[j, 0], queries.at[src_d, 2 * x + src_c], b_send.at[j, cc],
                b_recv.at[src_d, src_c], src_d, 2 * x + src_c,
            ).wait_recv()
        mine = queries.at[src_d, pl.ds(2 * x, 2)]
        fwd = remote(mine, mine, c_send.at[j], c_recv.at[src_d], d, 2 * (1 - x) + c)
        fwd.start()
        copies.append(fwd)

    arrive(0)
    remote(pvecs.at[1 - c], pvecs.at[1 - c], p_send, p_recv, d, 2 * x + 1 - c).wait_recv()
    for j in range(dp):
        if j + 1 < dp:
            arrive(j + 1)
        src_d = (d - j + dp) % dp
        other = queries.at[src_d, pl.ds(2 * (1 - x), 2)]
        remote(other, other, c_send.at[j], c_recv.at[src_d], d, 2 * (1 - x) + c).wait_recv()
        tokens = queries[src_d].reshape(mp * rows_b, emb)

        def score(g, carry):
            at = g * group
            passages = pvecs[at // own_p, pl.ds(pl.multiple_of((at % own_p) * pt, pt), group * pt), :]
            sims = lax.dot_general(
                passages, tokens, (((1,), (1,)), ((), ())), preferred_element_type=jnp.float32
            )
            weights = jnp.exp2(sims * (log2_e / softness)).reshape(group, pt, mp * rows_b)
            sums[pl.ds(pl.multiple_of(at, group), group), :] = jnp.sum(weights, axis=1)
            return carry

        lax.fori_loop(0, chip_p // group, score, 0)
        soft = softness * jnp.log(sums[...])
        student = lax.dot_general(
            fold, soft, (((1,), (1,)), ((), ())), precision=lax.Precision.HIGHEST,
            preferred_element_type=jnp.float32,
        )
        send_r[j, :, 0:chip_p] = student
        for i in range(mp):
            to = (m + i) % mp
            if j == 0 and i == 0:
                recv_r[d, m, :, 0:chip_p] = student
                continue
            cp = remote(
                send_r.at[j], recv_r.at[d, m], r_send.at[j, i], r_recv.at[d, m], src_d, to
            )
            cp.start()
            copies.append(cp)

    for j in range(dp):
        b = (d + j) % dp
        for i in range(mp):
            if j or i:
                src = (m + i) % mp
                remote(
                    send_r.at[j], recv_r.at[b, src], r_send.at[j, i], r_recv.at[b, src], b, src
                ).wait_recv()

    place = jnp.zeros((slots, qd), jnp.float32)
    for k in range(pick_count):
        place = place + jnp.where(slotq_ref[k:k + 1, :] == slot_row, 1.0, 0.0)
    cross = jnp.zeros((slots, 1), jnp.float32)
    mass = jnp.zeros((slots, 1), jnp.float32)
    for h in range(mp // 2):
        scores = recv_r[:, 2 * h:2 * h + 2, :, 0:chip_p].reshape(slots, chip_p)
        logp = lp_perm[:, h * chip_p:(h + 1) * chip_p]
        cross = cross + jnp.sum(jnp.exp(logp) * (logp - scores), axis=-1, keepdims=True)
        mass = mass + jnp.sum(jnp.exp(scores), axis=-1, keepdims=True)
    out_ref[...] = jnp.sum(place * cross, axis=0, keepdims=True) + jnp.log(
        jnp.sum(place * mass, axis=0, keepdims=True)
    )
    for cp in copies:
        cp.wait_send()


def fused_device(query_hidden, query_proj, passages, teacher, neg_blocks):
    dp, mp = lax.axis_size("dp"), lax.axis_size("mp")
    qd, picks = neg_blocks.shape
    qt = query_hidden.shape[1]
    emb = query_proj.shape[1]
    own_p, pt = passages.shape[0], passages.shape[1]
    cap = max(2, -(-(qd * picks) // dp))
    share = qt // mp
    half = cap // 2
    rows_b = half * share
    names = neg_blocks.T
    same = names[:, :, None, None] == names[None, None, :, :]
    order = jnp.arange(qd, dtype=jnp.int32)
    earlier = (order[None, :] < order[:, None])[None, :, None, :]
    rank = jnp.sum((same & earlier).astype(jnp.int32), axis=(2, 3))
    slotq = names * cap + rank
    slote = (slotq[:, :, None] * share + jnp.arange(share, dtype=jnp.int32)).reshape(
        picks, qd * share
    )
    vmem = pl.BlockSpec(memory_space=pltpu.VMEM)
    dma = pltpu.SemaphoreType.DMA
    loss = pl.pallas_call(
        functools.partial(fused_kernel, dp, mp, cap),
        out_shape=jax.ShapeDtypeStruct((1, qd), jnp.float32),
        in_specs=[vmem] * 6,
        out_specs=vmem,
        scratch_shapes=[
            pltpu.VMEM((mp, qd * share, emb), jnp.float32),
            pltpu.VMEM((mp, qd * share, emb), jnp.bfloat16),
            pltpu.VMEM((mp, qd * share, emb), jnp.bfloat16),
            pltpu.VMEM((2, own_p * pt, emb), jnp.bfloat16),
            pltpu.VMEM((dp, cap * share, qd * share), jnp.bfloat16),
            pltpu.VMEM((dp, 2, rows_b, emb), jnp.bfloat16),
            pltpu.VMEM((dp, mp, rows_b, emb), jnp.bfloat16),
            pltpu.VMEM((2 * own_p, mp * rows_b), jnp.float32),
            pltpu.VMEM((dp, half, 128), jnp.float32),
            pltpu.VMEM((dp, mp, half, 128), jnp.float32),
            pltpu.VMEM((dp * cap, teacher.shape[2]), jnp.float32),
            dma((mp,)), dma((mp,)), dma, dma, dma((dp, 2)), dma((dp, 2)),
            dma((dp,)), dma((dp,)), dma((dp, mp)), dma((dp, mp)),
        ],
        compiler_params=pltpu.CompilerParams(
            collective_id=0, has_side_effects=True, vmem_limit_bytes=40 * 2**20
        ),
    )(query_hidden, query_proj, passages, teacher, slotq, slote)
    return loss.reshape(qd)


def soft_scores(slot_rows, passage_vecs):
    slot_count = slot_rows.shape[0]
    block_size = 16
    padded_count = -(-slot_count // block_size) * block_size
    blocked = slot_rows.reshape(
        padded_count // block_size, block_size, slot_rows.shape[1], slot_rows.shape[2]
    )

    def block_scores(slot_block):
        sims = jnp.einsum(
            "sie,pje->sipj", slot_block, passage_vecs, preferred_element_type=jnp.float32
        )
        softened = softness * jnp.log(jnp.sum(jnp.exp(sims / softness), axis=-1))
        return jnp.sum(softened, axis=1)

    scored = lax.map(block_scores, blocked)
    return scored.reshape(padded_count, -1)


def per_device(query_hidden, query_proj, passages, teacher, neg_blocks):
    partial_sum = jnp.einsum(
        "qth,he->qte", query_hidden, query_proj, preferred_element_type=jnp.float32
    )
    passage_vecs = unit_rows(passages.astype(jnp.float32)).astype(jnp.bfloat16)
    dp_count = lax.axis_size("dp")
    query_count, pick_count = neg_blocks.shape
    embed_width = partial_sum.shape[2]
    row_count = query_count * pick_count
    capacity = max(2, -(-row_count // dp_count))
    slots_all = dp_count * capacity
    owners = neg_blocks.reshape(row_count)
    owner_hits = (owners[:, None] == jnp.arange(dp_count, dtype=jnp.int32)[None, :]).astype(
        jnp.int32
    )
    order = jnp.arange(row_count, dtype=jnp.int32)
    before = (order[None, :] < order[:, None]).astype(jnp.float32)
    earlier = jnp.dot(
        before, owner_hits.astype(jnp.float32), preferred_element_type=jnp.float32
    ).astype(jnp.int32)
    slot_rank = jnp.sum(earlier * owner_hits, axis=1)
    slot_ids = owners * capacity + slot_rank
    matches = (slot_ids[None, :] == jnp.arange(slots_all, dtype=jnp.int32)[:, None]).astype(
        jnp.int32
    )
    chosen = jnp.sum(matches.reshape(slots_all, query_count, pick_count), axis=2)
    token_share = lax.psum_scatter(partial_sum, "mp", scatter_dimension=1, tiled=True)
    share_vecs = unit_rows(token_share).astype(jnp.bfloat16)
    quarter = share_vecs.shape[1]
    token_part = jnp.einsum(
        "sq,qte->ste", chosen.astype(jnp.bfloat16), share_vecs, preferred_element_type=jnp.float32
    ).astype(jnp.bfloat16)
    token_part = token_part.reshape(dp_count, capacity, quarter, embed_width)
    arrived = lax.all_to_all(token_part, "dp", split_axis=0, concat_axis=0, tiled=True)
    joined = lax.all_gather(arrived, "mp", axis=2, tiled=True)
    tokens = joined.shape[2]
    scores = soft_scores(joined.reshape(slots_all, tokens, embed_width), passage_vecs).reshape(
        dp_count, capacity, -1
    )
    returned = lax.all_to_all(scores, "dp", split_axis=0, concat_axis=0, tiled=True)
    home_scores = returned.reshape(slots_all, -1)[slot_ids].reshape(query_count, pick_count, -1)
    teacher_logp = teacher - jnp.log(jnp.sum(jnp.exp(teacher), axis=(1, 2), keepdims=True))
    student = lax.all_gather(home_scores, "mp", axis=2, tiled=True)
    kl_loss = jnp.sum(jnp.exp(teacher_logp) * (teacher_logp - student), axis=(1, 2)) + jnp.log(
        jnp.sum(jnp.exp(student), axis=(1, 2))
    )
    return kl_loss


def solution(mesh):
    in_specs = (
        P("dp", None, "mp"),
        P("mp", None),
        P(("dp", "mp"), None, None),
        P("dp", None, None),
        P("dp", None),
    )
    out_specs = P("dp")
    dp, mp = mesh.shape["dp"], mesh.shape["mp"]

    def whole(query_hidden, query_proj, passages, teacher, neg_blocks):
        qd, picks = neg_blocks.shape[0] // dp, neg_blocks.shape[1]
        cap = max(2, -(-(qd * picks) // dp))
        share = query_hidden.shape[1] // mp
        own_p = passages.shape[0] // (dp * mp)
        fits = (
            mp == 4 and cap % 16 == 0 and share % 8 == 0 and own_p % group == 0
            and dp * mp <= 64
        )
        return jax.shard_map(
            fused_device if fits else per_device, mesh=mesh, in_specs=in_specs,
            out_specs=out_specs, check_vma=False,
        )(query_hidden, query_proj, passages, teacher, neg_blocks)

    return whole
```

```python
import functools
import jax
import jax.numpy as jnp
from jax import lax
from jax.experimental import pallas as pl
from jax.experimental.pallas import tpu as pltpu
from jax.sharding import PartitionSpec as P

softness = 0.1
log2_e = 1.4426950408889634


def unit_rows(values):
    return values * lax.rsqrt(jnp.sum(values * values, axis=-1, keepdims=True) + 1e-06)


def fused_kernel(
    dp, mp, cap,
    hid_hbm, proj_hbm, pas_hbm, teach_hbm, neg_hbm,
    out_ref,
    hid_ref, proj_ref, pas_ref, teach_ref, neg_ref,
    part, send_a, recv_a, pvecs, pick, send_b, queries, sums, send_r, recv_r, lp_perm, place,
    send_f, recv_f,
    loads, a_send, a_recv, p_send, p_recv, b_send, b_recv, r_send, r_recv, f_send, f_recv,
):
    d = lax.axis_index("dp")
    m = lax.axis_index("mp")
    x, c = m // 2, m % 2
    sib, across = 2 * x + 1 - c, 2 * (1 - x) + c
    far = 2 * (1 - x) + 1 - c
    qd, qt = hid_ref.shape[0], hid_ref.shape[1]
    emb = proj_ref.shape[1]
    picks = teach_ref.shape[1]
    share = qt // mp
    quarter = cap // mp
    rows_b = quarter * share
    own_p, pt = pas_ref.shape[0], pas_ref.shape[1]
    block_p = own_p * mp
    pairs = dp // 2

    def remote(src, dst, ssem, rsem, dd, mm):
        return pltpu.make_async_remote_copy(
            src_ref=src, dst_ref=dst, send_sem=ssem, recv_sem=rsem,
            device_id=(dd, mm), device_id_type=pl.DeviceIdType.MESH,
        )

    def partner(g, e, back):
        pair = (d // 2 - g + pairs) % pairs if back else (d // 2 + g) % pairs
        return 2 * pair + (d % 2 + e) % 2

    barrier = pltpu.get_barrier_semaphore()
    for j in range(dp):
        for i in range(mp):
            if j or i:
                pl.semaphore_signal(
                    barrier, inc=1, device_id=((d + j) % dp, (m + i) % mp),
                    device_id_type=pl.DeviceIdType.MESH,
                )
    inputs = []
    for k, (src, dst) in enumerate((
        (hid_hbm, hid_ref), (proj_hbm, proj_ref), (neg_hbm, neg_ref), (pas_hbm, pas_ref),
        (teach_hbm, teach_ref),
    )):
        cp = pltpu.make_async_copy(src, dst, loads.at[k])
        cp.start()
        inputs.append(cp)

    inputs[0].wait()
    inputs[1].wait()
    projected = jnp.dot(
        hid_ref[...].reshape(qd * qt, hid_ref.shape[2]), proj_ref[...],
        preferred_element_type=jnp.float32,
    ).reshape(qd, qt, emb)
    for k in range(mp):
        piece = projected[:, k * share:(k + 1) * share, :].reshape(qd * share, emb)
        part[k] = piece
        send_a[k] = piece.astype(jnp.bfloat16)
    inputs[3].wait()
    pvecs[m] = unit_rows(pas_ref[...].reshape(own_p * pt, emb).astype(jnp.float32)).astype(
        jnp.bfloat16
    )

    pl.semaphore_wait(barrier, dp * mp - 1)

    copies = []
    for i in range(1, mp):
        to = (m + i) % mp
        cp = remote(send_a.at[to], recv_a.at[m], a_send.at[i], a_recv.at[m], d, to)
        cp.start()
        copies.append(cp)
    for i, to in ((0, across), (1, sib)):
        cp = remote(pvecs.at[m], pvecs.at[m], p_send.at[i], p_recv.at[m], d, to)
        cp.start()
        copies.append(cp)

    inputs[2].wait()
    owner = lax.broadcasted_iota(jnp.int32, (qd, dp), 1)
    hits = [
        jnp.where(neg_ref[:, k:k + 1] == owner, 1.0, 0.0) for k in range(picks)
    ]
    row_q = lax.broadcasted_iota(jnp.int32, (qd, qd), 0)
    lane_q = lax.broadcasted_iota(jnp.int32, (qd, qd), 1)
    same = jnp.where(row_q == lane_q, 1.0, 0.0)
    before = jnp.where(row_q < lane_q, 1.0, 0.0)

    def turned(left, right):
        return lax.dot_general(
            left, right, (((0,), (0,)), ((), ())), preferred_element_type=jnp.float32
        )

    hits_t = [turned(h, same) for h in hits]
    rank = turned(sum(hits), before)
    code = jnp.where(sum(hits_t) > 0.5, rank, -1.0)
    spread = jnp.where(
        lax.broadcasted_iota(jnp.int32, (qd, qd * share), 1) // share
        == lax.broadcasted_iota(jnp.int32, (qd, qd * share), 0), 1.0, 0.0,
    )
    code_wide = jnp.dot(code, spread, preferred_element_type=jnp.float32)
    token = (lax.broadcasted_iota(jnp.int32, (dp, qd * share), 1) % share).astype(jnp.float32)
    code_wide = jnp.round(code_wide) * share + token
    row = lax.broadcasted_iota(jnp.int32, (cap * share, qd * share), 0).astype(jnp.float32)
    for b in range(dp):
        pick[b] = jnp.where(code_wide[b:b + 1, :] == row, 1.0, 0.0).astype(jnp.bfloat16)

    total = part[m]
    for i in range(1, mp):
        src = (m + i) % mp
        remote(send_a.at[src], recv_a.at[src], a_send.at[i], a_recv.at[src], d, src).wait_recv()
        total = total + recv_a[src].astype(jnp.float32)
    share_vecs = unit_rows(total).astype(jnp.bfloat16)

    for g in range(pairs):
        for e in range(2):
            b = partner(g, e, False)
            chosen = jnp.dot(pick[b], share_vecs, preferred_element_type=jnp.float32).astype(
                jnp.bfloat16
            )
            send_b[2 * g + e] = chosen.reshape(mp, rows_b, emb)
            for i in range(mp):
                to = (m + i) % mp
                if g == 0 and e == 0 and i == 0:
                    queries[d, m] = send_b[0, m]
                    continue
                cp = remote(
                    send_b.at[2 * g + e, to], queries.at[d, m], b_send.at[2 * g + e, i],
                    b_recv.at[d, m], b, to,
                )
                cp.start()
                copies.append(cp)

    inputs[4].wait()
    norm = jnp.zeros((qd, 1), jnp.float32)
    for k in range(picks):
        norm = norm + jnp.sum(jnp.exp(teach_ref[:, k, :]), axis=-1, keepdims=True)
    log_norm = jnp.log(norm)
    local = lax.broadcasted_iota(jnp.int32, (8, qd), 0)
    wanted = jnp.where(local < quarter, local + m * quarter, cap).astype(jnp.float32)
    perm = jnp.zeros((dp * 8, teach_ref.shape[2]), jnp.float32)
    spots = [jnp.where(code[b:b + 1, :] == wanted, 1.0, 0.0) for b in range(dp)]
    place[...] = jnp.concatenate(spots, axis=0)
    for k in range(picks):
        here = jnp.concatenate(
            [spots[b] * hits_t[k][b:b + 1, :] for b in range(dp)], axis=0
        )
        perm = perm + jnp.dot(
            here, teach_ref[:, k, :] - log_norm, precision=lax.Precision.HIGHEST,
            preferred_element_type=jnp.float32,
        )
    lp_perm[...] = perm

    lanes = mp * rows_b
    lane = lax.broadcasted_iota(jnp.int32, (16, 2 * lanes), 1)
    slot_of = lax.broadcasted_iota(jnp.int32, (16, 2 * lanes), 0)
    fold = jnp.where((lane // lanes) * 8 + (lane // share) % quarter == slot_of, 1.0, 0.0)

    def arrive(g):
        for e in range(2):
            src_d = partner(g, e, True)
            for i in range(mp):
                if g == 0 and e == 0 and i == 0:
                    continue
                src = (m + i) % mp
                remote(
                    send_b.at[2 * g + e, src], queries.at[src_d, src], b_send.at[2 * g + e, i],
                    b_recv.at[src_d, src], src_d, src,
                ).wait_recv()

    def score(g, side):
        tokens = jnp.concatenate(
            [queries[partner(g, e, True)].reshape(lanes, emb) for e in range(2)], axis=0
        )

        def one(h, carry):
            at = 2 * side + h
            sims = lax.dot_general(
                pvecs[at], tokens, (((1,), (1,)), ((), ())), preferred_element_type=jnp.float32
            )
            weights = jnp.exp2(sims * (log2_e / softness)).reshape(own_p, pt, 2 * lanes)
            sums[g, pl.ds(pl.multiple_of(at * own_p, own_p), own_p), :] = jnp.sum(weights, axis=1)
            return carry

        lax.fori_loop(0, 2, one, 0)

    def passages_from(src):
        remote(pvecs.at[src], pvecs.at[src], p_send.at[0], p_recv.at[src], d, across).wait_recv()

    arrive(0)
    passages_from(sib)
    score(0, x)
    for g in range(1, pairs):
        arrive(g)
        if g == min(2, pairs - 1):
            passages_from(across)
            cp = remote(pvecs.at[across], pvecs.at[across], p_send.at[2], p_recv.at[across], d, sib)
            cp.start()
            copies.append(cp)
        score(g, x)
    passages_from(far)
    for g in range(pairs):
        score(g, 1 - x)
        soft = softness * jnp.log(sums[g])
        student = lax.dot_general(
            fold, soft, (((1,), (1,)), ((), ())), precision=lax.Precision.HIGHEST,
            preferred_element_type=jnp.float32,
        )
        for e in range(2):
            piece = student[8 * e:8 * e + 8, :]
            if g == 0 and e == 0:
                recv_r[d, :, 0:block_p] = piece
                continue
            send_r[2 * g + e, :, 0:block_p] = piece
            cp = remote(
                send_r.at[2 * g + e], recv_r.at[d], r_send.at[2 * g + e], r_recv.at[d],
                partner(g, e, True), m,
            )
            cp.start()
            copies.append(cp)

    for g in range(pairs):
        for e in range(2):
            if g or e:
                b = partner(g, e, False)
                remote(
                    send_r.at[2 * g + e], recv_r.at[b], r_send.at[2 * g + e], r_recv.at[b], b, m
                ).wait_recv()

    scores = recv_r[:, :, 0:block_p].reshape(dp * 8, block_p)
    logp = lp_perm[...]
    cross = jnp.sum(jnp.exp(logp) * (logp - scores), axis=-1, keepdims=True)
    mass = jnp.sum(jnp.exp(scores), axis=-1, keepdims=True)
    send_f[0:1, 0:qd] = jnp.sum(place[...] * cross, axis=0, keepdims=True)
    send_f[1:2, 0:qd] = jnp.sum(place[...] * mass, axis=0, keepdims=True)
    for i in range(1, mp):
        to = (m + i) % mp
        cp = remote(send_f, recv_f.at[m], f_send.at[i], f_recv.at[m], d, to)
        cp.start()
        copies.append(cp)
    cross_q, mass_q = send_f[0:1, 0:qd], send_f[1:2, 0:qd]
    for i in range(1, mp):
        src = (m + i) % mp
        remote(send_f, recv_f.at[src], f_send.at[i], f_recv.at[src], d, src).wait_recv()
        cross_q = cross_q + recv_f[src, 0:1, 0:qd]
        mass_q = mass_q + recv_f[src, 1:2, 0:qd]
    out_ref[...] = cross_q + jnp.log(mass_q)
    for cp in copies:
        cp.wait_send()


def fused_device(query_hidden, query_proj, passages, teacher, neg_blocks):
    dp, mp = lax.axis_size("dp"), lax.axis_size("mp")
    qd, picks = neg_blocks.shape
    qt = query_hidden.shape[1]
    emb = query_proj.shape[1]
    own_p, pt = passages.shape[0], passages.shape[1]
    cap = max(2, -(-(qd * picks) // dp))
    share = qt // mp
    rows_b = cap // mp * share
    anywhere = pl.BlockSpec(memory_space=pl.ANY)
    dma = pltpu.SemaphoreType.DMA
    f32, bf16 = jnp.float32, jnp.bfloat16
    loss = pl.pallas_call(
        functools.partial(fused_kernel, dp, mp, cap),
        out_shape=jax.ShapeDtypeStruct((1, qd), f32),
        in_specs=[anywhere] * 5,
        out_specs=pl.BlockSpec(memory_space=pltpu.VMEM),
        scratch_shapes=[
            pltpu.VMEM(query_hidden.shape, bf16),
            pltpu.VMEM(query_proj.shape, bf16),
            pltpu.VMEM(passages.shape, bf16),
            pltpu.VMEM(teacher.shape, f32),
            pltpu.VMEM(neg_blocks.shape, jnp.int32),
            pltpu.VMEM((mp, qd * share, emb), f32),
            pltpu.VMEM((mp, qd * share, emb), bf16),
            pltpu.VMEM((mp, qd * share, emb), bf16),
            pltpu.VMEM((mp, own_p * pt, emb), bf16),
            pltpu.VMEM((dp, cap * share, qd * share), bf16),
            pltpu.VMEM((dp, mp, rows_b, emb), bf16),
            pltpu.VMEM((dp, mp, rows_b, emb), bf16),
            pltpu.VMEM((dp // 2, mp * own_p, 2 * mp * rows_b), f32),
            pltpu.VMEM((dp, 8, 128), f32),
            pltpu.VMEM((dp, 8, 128), f32),
            pltpu.VMEM((dp * 8, teacher.shape[2]), f32),
            pltpu.VMEM((dp * 8, qd), f32),
            pltpu.VMEM((8, 128), f32),
            pltpu.VMEM((mp, 8, 128), f32),
            dma((5,)), dma((mp,)), dma((mp,)), dma((3,)), dma((mp,)), dma((dp, mp)),
            dma((dp, mp)), dma((dp,)), dma((dp,)), dma((mp,)), dma((mp,)),
        ],
        compiler_params=pltpu.CompilerParams(
            collective_id=0, has_side_effects=True, vmem_limit_bytes=60 * 2**20
        ),
    )(query_hidden, query_proj, passages, teacher, neg_blocks)
    return loss.reshape(qd)


def soft_scores(slot_rows, passage_vecs):
    slot_count = slot_rows.shape[0]
    block_size = 16
    padded_count = -(-slot_count // block_size) * block_size
    blocked = slot_rows.reshape(
        padded_count // block_size, block_size, slot_rows.shape[1], slot_rows.shape[2]
    )

    def block_scores(slot_block):
        sims = jnp.einsum(
            "sie,pje->sipj", slot_block, passage_vecs, preferred_element_type=jnp.float32
        )
        softened = softness * jnp.log(jnp.sum(jnp.exp(sims / softness), axis=-1))
        return jnp.sum(softened, axis=1)

    scored = lax.map(block_scores, blocked)
    return scored.reshape(padded_count, -1)


def per_device(query_hidden, query_proj, passages, teacher, neg_blocks):
    partial_sum = jnp.einsum(
        "qth,he->qte", query_hidden, query_proj, preferred_element_type=jnp.float32
    )
    passage_vecs = unit_rows(passages.astype(jnp.float32)).astype(jnp.bfloat16)
    dp_count = lax.axis_size("dp")
    query_count, pick_count = neg_blocks.shape
    embed_width = partial_sum.shape[2]
    row_count = query_count * pick_count
    capacity = max(2, -(-row_count // dp_count))
    slots_all = dp_count * capacity
    owners = neg_blocks.reshape(row_count)
    owner_hits = (owners[:, None] == jnp.arange(dp_count, dtype=jnp.int32)[None, :]).astype(
        jnp.int32
    )
    order = jnp.arange(row_count, dtype=jnp.int32)
    before = (order[None, :] < order[:, None]).astype(jnp.float32)
    earlier = jnp.dot(
        before, owner_hits.astype(jnp.float32), preferred_element_type=jnp.float32
    ).astype(jnp.int32)
    slot_rank = jnp.sum(earlier * owner_hits, axis=1)
    slot_ids = owners * capacity + slot_rank
    matches = (slot_ids[None, :] == jnp.arange(slots_all, dtype=jnp.int32)[:, None]).astype(
        jnp.int32
    )
    chosen = jnp.sum(matches.reshape(slots_all, query_count, pick_count), axis=2)
    token_share = lax.psum_scatter(partial_sum, "mp", scatter_dimension=1, tiled=True)
    share_vecs = unit_rows(token_share).astype(jnp.bfloat16)
    quarter = share_vecs.shape[1]
    token_part = jnp.einsum(
        "sq,qte->ste", chosen.astype(jnp.bfloat16), share_vecs, preferred_element_type=jnp.float32
    ).astype(jnp.bfloat16)
    token_part = token_part.reshape(dp_count, capacity, quarter, embed_width)
    arrived = lax.all_to_all(token_part, "dp", split_axis=0, concat_axis=0, tiled=True)
    joined = lax.all_gather(arrived, "mp", axis=2, tiled=True)
    tokens = joined.shape[2]
    scores = soft_scores(joined.reshape(slots_all, tokens, embed_width), passage_vecs).reshape(
        dp_count, capacity, -1
    )
    returned = lax.all_to_all(scores, "dp", split_axis=0, concat_axis=0, tiled=True)
    home_scores = returned.reshape(slots_all, -1)[slot_ids].reshape(query_count, pick_count, -1)
    teacher_logp = teacher - jnp.log(jnp.sum(jnp.exp(teacher), axis=(1, 2), keepdims=True))
    student = lax.all_gather(home_scores, "mp", axis=2, tiled=True)
    kl_loss = jnp.sum(jnp.exp(teacher_logp) * (teacher_logp - student), axis=(1, 2)) + jnp.log(
        jnp.sum(jnp.exp(student), axis=(1, 2))
    )
    return kl_loss


def solution(mesh):
    in_specs = (
        P("dp", None, "mp"),
        P("mp", None),
        P(("dp", "mp"), None, None),
        P("dp", None, None),
        P("dp", None),
    )
    out_specs = P("dp")
    dp, mp = mesh.shape["dp"], mesh.shape["mp"]

    def whole(query_hidden, query_proj, passages, teacher, neg_blocks):
        qd, picks = neg_blocks.shape[0] // dp, neg_blocks.shape[1]
        cap = max(2, -(-(qd * picks) // dp))
        share = query_hidden.shape[1] // mp
        own_p = passages.shape[0] // (dp * mp)
        fits = (
            mp == 4 and dp % 2 == 0 and dp * mp <= 64 and share % 8 == 0
            and cap % mp == 0 and cap // mp <= 8 and (cap // mp * share) % 16 == 0
            and own_p % 8 == 0 and own_p * mp <= 128 and cap <= 256
        )
        return jax.shard_map(
            fused_device if fits else per_device, mesh=mesh, in_specs=in_specs,
            out_specs=out_specs, check_vma=False,
        )(query_hidden, query_proj, passages, teacher, neg_blocks)

    return whole
```

```python
import functools
import jax
import jax.numpy as jnp
from jax import lax
from jax.experimental import pallas as pl
from jax.experimental.pallas import tpu as pltpu
from jax.sharding import PartitionSpec as P

softness = 0.1
log2_e = 1.4426950408889634


def unit_rows(values):
    return values * lax.rsqrt(jnp.sum(values * values, axis=-1, keepdims=True) + 1e-06)


def fused_kernel(
    dp, mp, cap,
    hid_hbm, proj_hbm, pas_hbm, teach_hbm, neg_hbm,
    out_ref,
    hid_ref, proj_ref, pas_ref, teach_ref, neg_ref,
    part, send_a, recv_a, pvecs, pick, send_b, queries, sums, send_r, recv_r, lp_perm, place,
    loads, a_send, a_recv, p_send, p_recv, b_send, b_recv, c_send, c_recv, r_send, r_recv,
):
    d = lax.axis_index("dp")
    m = lax.axis_index("mp")
    x, c = m // 2, m % 2
    sib, across = 2 * x + 1 - c, 2 * (1 - x) + c
    qd, qt = hid_ref.shape[0], hid_ref.shape[1]
    emb = proj_ref.shape[1]
    picks = teach_ref.shape[1]
    share = qt // mp
    half = cap // 2
    rows_b = half * share
    own_p, pt = pas_ref.shape[0], pas_ref.shape[1]
    chip_p = 2 * own_p
    slots = dp * cap
    direct = min(2, dp)

    def remote(src, dst, ssem, rsem, dd, mm):
        return pltpu.make_async_remote_copy(
            src_ref=src, dst_ref=dst, send_sem=ssem, recv_sem=rsem,
            device_id=(dd, mm), device_id_type=pl.DeviceIdType.MESH,
        )

    def partner(j):
        at, bit = d, 1
        while bit <= j:
            if j & bit:
                at = at + bit - 2 * bit * ((d // bit) % 2)
            bit = 2 * bit
        return at

    barrier = pltpu.get_barrier_semaphore()
    for j in range(dp):
        for i in range(mp):
            if j or i:
                pl.semaphore_signal(
                    barrier, inc=1, device_id=((d + j) % dp, (m + i) % mp),
                    device_id_type=pl.DeviceIdType.MESH,
                )
    inputs = []
    for k, (src, dst) in enumerate((
        (hid_hbm, hid_ref), (proj_hbm, proj_ref), (neg_hbm, neg_ref), (pas_hbm, pas_ref),
        (teach_hbm, teach_ref),
    )):
        cp = pltpu.make_async_copy(src, dst, loads.at[k])
        cp.start()
        inputs.append(cp)

    inputs[0].wait()
    inputs[1].wait()
    projected = jnp.dot(
        hid_ref[...].reshape(qd * qt, hid_ref.shape[2]), proj_ref[...],
        preferred_element_type=jnp.float32,
    ).reshape(qd, qt, emb)
    for k in range(mp):
        piece = projected[:, k * share:(k + 1) * share, :].reshape(qd * share, emb)
        part[k] = piece
        send_a[k] = piece.astype(jnp.bfloat16)
    inputs[3].wait()
    pvecs[c] = unit_rows(pas_ref[...].reshape(own_p * pt, emb).astype(jnp.float32)).astype(
        jnp.bfloat16
    )

    pl.semaphore_wait(barrier, dp * mp - 1)

    copies = []
    for i in range(1, mp):
        to = (m + i) % mp
        cp = remote(send_a.at[to], recv_a.at[m], a_send.at[i], a_recv.at[m], d, to)
        cp.start()
        copies.append(cp)
    cp = remote(pvecs.at[c], pvecs.at[c], p_send, p_recv, d, sib)
    cp.start()
    copies.append(cp)

    inputs[2].wait()
    owner = lax.broadcasted_iota(jnp.int32, (dp, qd), 0)
    hits_t = [jnp.where(neg_ref[k:k + 1, :] == owner, 1.0, 0.0) for k in range(picks)]
    before = jnp.where(
        lax.broadcasted_iota(jnp.int32, (qd, qd), 0)
        < lax.broadcasted_iota(jnp.int32, (qd, qd), 1), 1.0, 0.0,
    )
    rank = jnp.dot(sum(hits_t), before, preferred_element_type=jnp.float32)
    code = jnp.where(sum(hits_t) > 0.5, rank, -1.0)
    spread = jnp.where(
        lax.broadcasted_iota(jnp.int32, (qd, qd * share), 1) // share
        == lax.broadcasted_iota(jnp.int32, (qd, qd * share), 0), 1.0, 0.0,
    )
    code_wide = jnp.dot(code, spread, preferred_element_type=jnp.float32)
    token = (lax.broadcasted_iota(jnp.int32, (dp, qd * share), 1) % share).astype(jnp.float32)
    code_wide = jnp.round(code_wide) * share + token
    row = lax.broadcasted_iota(jnp.int32, (cap * share, qd * share), 0).astype(jnp.float32)
    for b in range(dp):
        pick[b] = jnp.where(code_wide[b:b + 1, :] == row, 1.0, 0.0).astype(jnp.bfloat16)

    peers = ((m, c), (sib, 1 - c), (across, c), (2 * (1 - x) + 1 - c, 1 - c))
    total = part[m]
    for i in range(1, mp):
        src = (m + i) % mp
        remote(send_a.at[src], recv_a.at[src], a_send.at[i], a_recv.at[src], d, src).wait_recv()
        total = total + recv_a[src].astype(jnp.float32)
    share_vecs = unit_rows(total).astype(jnp.bfloat16)

    for j in range(dp):
        b = partner(j)
        chosen = jnp.dot(pick[b], share_vecs, preferred_element_type=jnp.float32).astype(
            jnp.bfloat16
        )
        send_b[j] = chosen.reshape(2, rows_b, emb)
        for i, (to, half_of) in enumerate(peers[:mp if j < direct else 2]):
            if j == 0 and i == 0:
                queries[d, m] = send_b[0, c]
                continue
            cp = remote(
                send_b.at[j, half_of], queries.at[d, m], b_send.at[j, i], b_recv.at[d, m], b, to
            )
            cp.start()
            copies.append(cp)

    inputs[4].wait()
    norm = jnp.zeros((qd, 1), jnp.float32)
    for k in range(picks):
        norm = norm + jnp.sum(jnp.exp(teach_ref[:, k, :]), axis=-1, keepdims=True)
    log_norm = jnp.log(norm)
    local = lax.broadcasted_iota(jnp.int32, (cap, qd), 0).astype(jnp.float32)
    perm = jnp.zeros((slots, teach_ref.shape[2]), jnp.float32)
    spots = [jnp.where(code[b:b + 1, :] == local, 1.0, 0.0) for b in range(dp)]
    place[...] = jnp.concatenate(spots, axis=0)
    for k in range(picks):
        here = jnp.concatenate(
            [spots[b] * hits_t[k][b:b + 1, :] for b in range(dp)], axis=0
        )
        perm = perm + jnp.dot(
            here, teach_ref[:, k, :] - log_norm, precision=lax.Precision.HIGHEST,
            preferred_element_type=jnp.float32,
        )
    lp_perm[...] = perm

    lanes = mp * rows_b
    lane = lax.broadcasted_iota(jnp.int32, (half, lanes), 1)
    slot_of = lax.broadcasted_iota(jnp.int32, (half, lanes), 0)
    fold = jnp.where((lane // share) % half == slot_of, 1.0, 0.0)

    def arrive(j):
        src_d = partner(j)
        for i, (src, _) in enumerate(peers[:mp if j < direct else 2]):
            if j == 0 and i == 0:
                continue
            remote(
                send_b.at[j, 0], queries.at[src_d, src], b_send.at[j, i], b_recv.at[src_d, src],
                src_d, src,
            ).wait_recv()
        if j >= direct:
            mine = queries.at[src_d, pl.ds(2 * x, 2)]
            fwd = remote(mine, mine, c_send.at[j], c_recv.at[src_d], d, across)
            fwd.start()
            copies.append(fwd)

    def complete(j):
        if j >= direct:
            src_d = partner(j)
            other = queries.at[src_d, pl.ds(2 * (1 - x), 2)]
            remote(other, other, c_send.at[j], c_recv.at[src_d], d, across).wait_recv()

    def score(j):
        tokens = queries[partner(j)].reshape(lanes, emb)

        def one(at, carry):
            sims = lax.dot_general(
                pvecs[at], tokens, (((1,), (1,)), ((), ())), preferred_element_type=jnp.float32
            )
            weights = jnp.exp2(sims * (log2_e / softness)).reshape(own_p, pt, lanes)
            sums[pl.ds(pl.multiple_of(at * own_p, own_p), own_p), :] = jnp.sum(weights, axis=1)
            return carry

        lax.fori_loop(0, 2, one, 0)

    arrive(0)
    remote(pvecs.at[1 - c], pvecs.at[1 - c], p_send, p_recv, d, sib).wait_recv()
    ahead = 1
    for j in range(dp):
        while ahead < dp and ahead <= j + 2:
            arrive(ahead)
            ahead = ahead + 1
        complete(j)
        score(j)
        soft = softness * jnp.log(sums[...])
        student = lax.dot_general(
            fold, soft, (((1,), (1,)), ((), ())), precision=lax.Precision.HIGHEST,
            preferred_element_type=jnp.float32,
        )
        send_r[j, :, 0:chip_p] = student
        for i in range(mp):
            to = (m + i) % mp
            if j == 0 and i == 0:
                recv_r[d, m, :, 0:chip_p] = student
                continue
            cp = remote(
                send_r.at[j], recv_r.at[d, m], r_send.at[j, i], r_recv.at[d, m], partner(j), to
            )
            cp.start()
            copies.append(cp)

    for j in range(dp):
        b = partner(j)
        for i in range(mp):
            if j or i:
                src = (m + i) % mp
                remote(
                    send_r.at[j], recv_r.at[b, src], r_send.at[j, i], r_recv.at[b, src], b, src
                ).wait_recv()

    cross = jnp.zeros((slots, 1), jnp.float32)
    mass = jnp.zeros((slots, 1), jnp.float32)
    for h in range(mp // 2):
        scores = recv_r[:, 2 * h:2 * h + 2, :, 0:chip_p].reshape(slots, chip_p)
        logp = lp_perm[:, h * chip_p:(h + 1) * chip_p]
        cross = cross + jnp.sum(jnp.exp(logp) * (logp - scores), axis=-1, keepdims=True)
        mass = mass + jnp.sum(jnp.exp(scores), axis=-1, keepdims=True)
    out_ref[...] = jnp.sum(place[...] * cross, axis=0, keepdims=True) + jnp.log(
        jnp.sum(place[...] * mass, axis=0, keepdims=True)
    )
    for cp in copies:
        cp.wait_send()


def fused_device(query_hidden, query_proj, passages, teacher, neg_blocks):
    dp, mp = lax.axis_size("dp"), lax.axis_size("mp")
    qd, picks = neg_blocks.shape
    qt = query_hidden.shape[1]
    emb = query_proj.shape[1]
    own_p, pt = passages.shape[0], passages.shape[1]
    cap = max(2, -(-(qd * picks) // dp))
    share = qt // mp
    half = cap // 2
    rows_b = half * share
    anywhere = pl.BlockSpec(memory_space=pl.ANY)
    dma = pltpu.SemaphoreType.DMA
    f32, bf16 = jnp.float32, jnp.bfloat16
    loss = pl.pallas_call(
        functools.partial(fused_kernel, dp, mp, cap),
        out_shape=jax.ShapeDtypeStruct((1, qd), f32),
        in_specs=[anywhere] * 5,
        out_specs=pl.BlockSpec(memory_space=pltpu.VMEM),
        scratch_shapes=[
            pltpu.VMEM(query_hidden.shape, bf16),
            pltpu.VMEM(query_proj.shape, bf16),
            pltpu.VMEM(passages.shape, bf16),
            pltpu.VMEM(teacher.shape, f32),
            pltpu.VMEM((picks, qd), jnp.int32),
            pltpu.VMEM((mp, qd * share, emb), f32),
            pltpu.VMEM((mp, qd * share, emb), bf16),
            pltpu.VMEM((mp, qd * share, emb), bf16),
            pltpu.VMEM((2, own_p * pt, emb), bf16),
            pltpu.VMEM((dp, cap * share, qd * share), bf16),
            pltpu.VMEM((dp, 2, rows_b, emb), bf16),
            pltpu.VMEM((dp, mp, rows_b, emb), bf16),
            pltpu.VMEM((2 * own_p, mp * rows_b), f32),
            pltpu.VMEM((dp, half, 128), f32),
            pltpu.VMEM((dp, mp, half, 128), f32),
            pltpu.VMEM((dp * cap, teacher.shape[2]), f32),
            pltpu.VMEM((dp * cap, qd), f32),
            dma((5,)), dma((mp,)), dma((mp,)), dma, dma, dma((dp, mp)), dma((dp, mp)),
            dma((dp,)), dma((dp,)), dma((dp, mp)), dma((dp, mp)),
        ],
        compiler_params=pltpu.CompilerParams(
            collective_id=0, has_side_effects=True, vmem_limit_bytes=60 * 2**20
        ),
    )(query_hidden, query_proj, passages, teacher, neg_blocks.T)
    return loss.reshape(qd)


def soft_scores(slot_rows, passage_vecs):
    slot_count = slot_rows.shape[0]
    block_size = 16
    padded_count = -(-slot_count // block_size) * block_size
    blocked = slot_rows.reshape(
        padded_count // block_size, block_size, slot_rows.shape[1], slot_rows.shape[2]
    )

    def block_scores(slot_block):
        sims = jnp.einsum(
            "sie,pje->sipj", slot_block, passage_vecs, preferred_element_type=jnp.float32
        )
        softened = softness * jnp.log(jnp.sum(jnp.exp(sims / softness), axis=-1))
        return jnp.sum(softened, axis=1)

    scored = lax.map(block_scores, blocked)
    return scored.reshape(padded_count, -1)


def per_device(query_hidden, query_proj, passages, teacher, neg_blocks):
    partial_sum = jnp.einsum(
        "qth,he->qte", query_hidden, query_proj, preferred_element_type=jnp.float32
    )
    passage_vecs = unit_rows(passages.astype(jnp.float32)).astype(jnp.bfloat16)
    dp_count = lax.axis_size("dp")
    query_count, pick_count = neg_blocks.shape
    embed_width = partial_sum.shape[2]
    row_count = query_count * pick_count
    capacity = max(2, -(-row_count // dp_count))
    slots_all = dp_count * capacity
    owners = neg_blocks.reshape(row_count)
    owner_hits = (owners[:, None] == jnp.arange(dp_count, dtype=jnp.int32)[None, :]).astype(
        jnp.int32
    )
    order = jnp.arange(row_count, dtype=jnp.int32)
    before = (order[None, :] < order[:, None]).astype(jnp.float32)
    earlier = jnp.dot(
        before, owner_hits.astype(jnp.float32), preferred_element_type=jnp.float32
    ).astype(jnp.int32)
    slot_rank = jnp.sum(earlier * owner_hits, axis=1)
    slot_ids = owners * capacity + slot_rank
    matches = (slot_ids[None, :] == jnp.arange(slots_all, dtype=jnp.int32)[:, None]).astype(
        jnp.int32
    )
    chosen = jnp.sum(matches.reshape(slots_all, query_count, pick_count), axis=2)
    token_share = lax.psum_scatter(partial_sum, "mp", scatter_dimension=1, tiled=True)
    share_vecs = unit_rows(token_share).astype(jnp.bfloat16)
    quarter = share_vecs.shape[1]
    token_part = jnp.einsum(
        "sq,qte->ste", chosen.astype(jnp.bfloat16), share_vecs, preferred_element_type=jnp.float32
    ).astype(jnp.bfloat16)
    token_part = token_part.reshape(dp_count, capacity, quarter, embed_width)
    arrived = lax.all_to_all(token_part, "dp", split_axis=0, concat_axis=0, tiled=True)
    joined = lax.all_gather(arrived, "mp", axis=2, tiled=True)
    tokens = joined.shape[2]
    scores = soft_scores(joined.reshape(slots_all, tokens, embed_width), passage_vecs).reshape(
        dp_count, capacity, -1
    )
    returned = lax.all_to_all(scores, "dp", split_axis=0, concat_axis=0, tiled=True)
    home_scores = returned.reshape(slots_all, -1)[slot_ids].reshape(query_count, pick_count, -1)
    teacher_logp = teacher - jnp.log(jnp.sum(jnp.exp(teacher), axis=(1, 2), keepdims=True))
    student = lax.all_gather(home_scores, "mp", axis=2, tiled=True)
    kl_loss = jnp.sum(jnp.exp(teacher_logp) * (teacher_logp - student), axis=(1, 2)) + jnp.log(
        jnp.sum(jnp.exp(student), axis=(1, 2))
    )
    return kl_loss


def solution(mesh):
    in_specs = (
        P("dp", None, "mp"),
        P("mp", None),
        P(("dp", "mp"), None, None),
        P("dp", None, None),
        P("dp", None),
    )
    out_specs = P("dp")
    dp, mp = mesh.shape["dp"], mesh.shape["mp"]

    def whole(query_hidden, query_proj, passages, teacher, neg_blocks):
        qd, picks = neg_blocks.shape[0] // dp, neg_blocks.shape[1]
        cap = max(2, -(-(qd * picks) // dp))
        share = query_hidden.shape[1] // mp
        own_p = passages.shape[0] // (dp * mp)
        fits = (
            mp == 4 and dp & (dp - 1) == 0 and dp * mp <= 64 and share % 8 == 0
            and cap % 16 == 0 and cap <= 256 and own_p % 8 == 0 and own_p <= 64
        )
        return jax.shard_map(
            fused_device if fits else per_device, mesh=mesh, in_specs=in_specs,
            out_specs=out_specs, check_vma=False,
        )(query_hidden, query_proj, passages, teacher, neg_blocks)

    return whole
```

```python
import functools
import jax
import jax.numpy as jnp
from jax import lax
from jax.experimental import pallas as pl
from jax.experimental.pallas import tpu as pltpu
from jax.sharding import PartitionSpec as P

softness = 0.1
log2_e = 1.4426950408889634


def unit_rows(values):
    return values * lax.rsqrt(jnp.sum(values * values, axis=-1, keepdims=True) + 1e-06)


def fused_kernel(
    dp, mp, cap,
    hid_hbm, proj_hbm, pas_hbm, teach_hbm, neg_hbm,
    out_ref,
    hid_ref, proj_ref, pas_ref, teach_ref, neg_ref,
    part, send_a, recv_a, pvecs, pick, send_b, queries, sums, send_r, recv_r, lp_perm, place,
    loads, a_send, a_recv, p_send, p_recv, b_send, b_recv, c_send, c_recv, r_send, r_recv,
):
    d = lax.axis_index("dp")
    m = lax.axis_index("mp")
    x, c = m // 2, m % 2
    sib, across = 2 * x + 1 - c, 2 * (1 - x) + c
    qd, qt = hid_ref.shape[0], hid_ref.shape[1]
    emb = proj_ref.shape[1]
    picks = teach_ref.shape[1]
    share = qt // mp
    half = cap // 2
    rows_b = half * share
    own_p, pt = pas_ref.shape[0], pas_ref.shape[1]
    chip_p = 2 * own_p
    slots = dp * cap
    direct = min(2, dp)

    def remote(src, dst, ssem, rsem, dd, mm):
        return pltpu.make_async_remote_copy(
            src_ref=src, dst_ref=dst, send_sem=ssem, recv_sem=rsem,
            device_id=(dd, mm), device_id_type=pl.DeviceIdType.MESH,
        )

    def partner(j):
        at, bit = d, 1
        while bit <= j:
            if j & bit:
                at = at + bit - 2 * bit * ((d // bit) % 2)
            bit = 2 * bit
        return at

    barrier = pltpu.get_barrier_semaphore()
    for j in range(dp):
        for i in range(mp):
            if j or i:
                pl.semaphore_signal(
                    barrier, inc=1, device_id=((d + j) % dp, (m + i) % mp),
                    device_id_type=pl.DeviceIdType.MESH,
                )
    inputs = []
    for k, (src, dst) in enumerate((
        (hid_hbm, hid_ref), (proj_hbm, proj_ref), (neg_hbm, neg_ref), (pas_hbm, pas_ref),
        (teach_hbm, teach_ref),
    )):
        cp = pltpu.make_async_copy(src, dst, loads.at[k])
        cp.start()
        inputs.append(cp)

    inputs[0].wait()
    inputs[1].wait()
    projected = jnp.dot(
        hid_ref[...].reshape(qd * qt, hid_ref.shape[2]), proj_ref[...],
        preferred_element_type=jnp.float32,
    ).reshape(qd, qt, emb)
    for k in range(mp):
        piece = projected[:, k * share:(k + 1) * share, :].reshape(qd * share, emb)
        part[k] = piece
        send_a[k] = piece.astype(jnp.bfloat16)
    inputs[3].wait()
    pvecs[c] = unit_rows(pas_ref[...].reshape(own_p * pt, emb).astype(jnp.float32)).astype(
        jnp.bfloat16
    )

    pl.semaphore_wait(barrier, dp * mp - 1)

    copies = []
    for i in range(1, mp):
        to = (m + i) % mp
        cp = remote(send_a.at[to], recv_a.at[m], a_send.at[i], a_recv.at[m], d, to)
        cp.start()
        copies.append(cp)
    cp = remote(pvecs.at[c], pvecs.at[c], p_send, p_recv, d, sib)
    cp.start()
    copies.append(cp)

    inputs[2].wait()
    owner = lax.broadcasted_iota(jnp.int32, (dp, qd), 0)
    hits_t = [jnp.where(neg_ref[k:k + 1, :] == owner, 1.0, 0.0) for k in range(picks)]
    before = jnp.where(
        lax.broadcasted_iota(jnp.int32, (qd, qd), 0)
        < lax.broadcasted_iota(jnp.int32, (qd, qd), 1), 1.0, 0.0,
    )
    rank = jnp.dot(sum(hits_t), before, preferred_element_type=jnp.float32)
    code = jnp.where(sum(hits_t) > 0.5, rank, -1.0)
    spread = jnp.where(
        lax.broadcasted_iota(jnp.int32, (qd, qd * share), 1) // share
        == lax.broadcasted_iota(jnp.int32, (qd, qd * share), 0), 1.0, 0.0,
    )
    code_wide = jnp.dot(code, spread, preferred_element_type=jnp.float32)
    token = (lax.broadcasted_iota(jnp.int32, (dp, qd * share), 1) % share).astype(jnp.float32)
    code_wide = jnp.round(code_wide) * share + token
    row = lax.broadcasted_iota(jnp.int32, (cap * share, qd * share), 0).astype(jnp.float32)
    for b in range(dp):
        pick[b] = jnp.where(code_wide[b:b + 1, :] == row, 1.0, 0.0).astype(jnp.bfloat16)

    peers = ((m, c), (sib, 1 - c), (across, c), (2 * (1 - x) + 1 - c, 1 - c))
    total = part[m]
    for i in range(1, mp):
        src = (m + i) % mp
        remote(send_a.at[src], recv_a.at[src], a_send.at[i], a_recv.at[src], d, src).wait_recv()
        total = total + recv_a[src].astype(jnp.float32)
    share_vecs = unit_rows(total).astype(jnp.bfloat16)

    for j in range(dp):
        b = partner(j)
        chosen = jnp.dot(pick[b], share_vecs, preferred_element_type=jnp.float32).astype(
            jnp.bfloat16
        )
        send_b[j] = chosen.reshape(2, rows_b, emb)
        for i, (to, half_of) in enumerate(peers[:mp if j < direct else 2]):
            if j == 0 and i == 0:
                queries[d, m] = send_b[0, c]
                continue
            cp = remote(
                send_b.at[j, half_of], queries.at[d, m], b_send.at[j, i], b_recv.at[d, m], b, to
            )
            cp.start()
            copies.append(cp)

    inputs[4].wait()
    norm = jnp.zeros((qd, 1), jnp.float32)
    for k in range(picks):
        norm = norm + jnp.sum(jnp.exp(teach_ref[:, k, :]), axis=-1, keepdims=True)
    log_norm = jnp.log(norm)
    local = lax.broadcasted_iota(jnp.int32, (cap, qd), 0).astype(jnp.float32)
    perm = jnp.zeros((slots, teach_ref.shape[2]), jnp.float32)
    spots = [jnp.where(code[b:b + 1, :] == local, 1.0, 0.0) for b in range(dp)]
    place[...] = jnp.concatenate(spots, axis=0)
    for k in range(picks):
        here = jnp.concatenate(
            [spots[b] * hits_t[k][b:b + 1, :] for b in range(dp)], axis=0
        )
        perm = perm + jnp.dot(
            here, teach_ref[:, k, :] - log_norm, precision=lax.Precision.HIGHEST,
            preferred_element_type=jnp.float32,
        )
    lp_perm[...] = perm

    lanes = mp * rows_b
    lane = lax.broadcasted_iota(jnp.int32, (half, lanes), 1)
    slot_of = lax.broadcasted_iota(jnp.int32, (half, lanes), 0)
    fold = jnp.where((lane // share) % half == slot_of, 1.0, 0.0)

    def arrive(j):
        src_d = partner(j)
        for i, (src, _) in enumerate(peers[:mp if j < direct else 2]):
            if j == 0 and i == 0:
                continue
            remote(
                send_b.at[j, 0], queries.at[src_d, src], b_send.at[j, i], b_recv.at[src_d, src],
                src_d, src,
            ).wait_recv()
        if j >= direct:
            mine = queries.at[src_d, pl.ds(2 * x, 2)]
            fwd = remote(mine, mine, c_send.at[j], c_recv.at[src_d], d, across)
            fwd.start()
            copies.append(fwd)

    def complete(j):
        if j >= direct:
            src_d = partner(j)
            other = queries.at[src_d, pl.ds(2 * (1 - x), 2)]
            remote(other, other, c_send.at[j], c_recv.at[src_d], d, across).wait_recv()

    def score(j):
        tokens = queries[partner(j)].reshape(lanes, emb)

        def one(at, carry):
            sims = lax.dot_general(
                pvecs[at], tokens, (((1,), (1,)), ((), ())), preferred_element_type=jnp.float32
            )
            weights = jnp.exp2(sims * (log2_e / softness)).reshape(own_p, pt, lanes)
            sums[pl.ds(pl.multiple_of(at * own_p, own_p), own_p), :] = jnp.sum(weights, axis=1)
            return carry

        lax.fori_loop(0, 2, one, 0)

    arrive(0)
    remote(pvecs.at[1 - c], pvecs.at[1 - c], p_send, p_recv, d, sib).wait_recv()
    ahead = 1
    for j in range(dp):
        while ahead < dp and ahead <= j + 4:
            arrive(ahead)
            ahead = ahead + 1
        complete(j)
        score(j)
        soft = softness * jnp.log(sums[...])
        student = lax.dot_general(
            fold, soft, (((1,), (1,)), ((), ())), precision=lax.Precision.HIGHEST,
            preferred_element_type=jnp.float32,
        )
        send_r[j, :, 0:chip_p] = student
        for i in range(mp):
            to = (m + i) % mp
            if j == 0 and i == 0:
                recv_r[d, m, :, 0:chip_p] = student
                continue
            cp = remote(
                send_r.at[j], recv_r.at[d, m], r_send.at[j, i], r_recv.at[d, m], partner(j), to
            )
            cp.start()
            copies.append(cp)

    for j in range(dp):
        b = partner(j)
        for i in range(mp):
            if j or i:
                src = (m + i) % mp
                remote(
                    send_r.at[j], recv_r.at[b, src], r_send.at[j, i], r_recv.at[b, src], b, src
                ).wait_recv()

    cross = jnp.zeros((slots, 1), jnp.float32)
    mass = jnp.zeros((slots, 1), jnp.float32)
    for h in range(mp // 2):
        scores = recv_r[:, 2 * h:2 * h + 2, :, 0:chip_p].reshape(slots, chip_p)
        logp = lp_perm[:, h * chip_p:(h + 1) * chip_p]
        cross = cross + jnp.sum(jnp.exp(logp) * (logp - scores), axis=-1, keepdims=True)
        mass = mass + jnp.sum(jnp.exp(scores), axis=-1, keepdims=True)
    out_ref[...] = jnp.sum(place[...] * cross, axis=0, keepdims=True) + jnp.log(
        jnp.sum(place[...] * mass, axis=0, keepdims=True)
    )
    for cp in copies:
        cp.wait_send()


def fused_device(query_hidden, query_proj, passages, teacher, neg_blocks):
    dp, mp = lax.axis_size("dp"), lax.axis_size("mp")
    qd, picks = neg_blocks.shape
    qt = query_hidden.shape[1]
    emb = query_proj.shape[1]
    own_p, pt = passages.shape[0], passages.shape[1]
    cap = max(2, -(-(qd * picks) // dp))
    share = qt // mp
    half = cap // 2
    rows_b = half * share
    anywhere = pl.BlockSpec(memory_space=pl.ANY)
    dma = pltpu.SemaphoreType.DMA
    f32, bf16 = jnp.float32, jnp.bfloat16
    loss = pl.pallas_call(
        functools.partial(fused_kernel, dp, mp, cap),
        out_shape=jax.ShapeDtypeStruct((1, qd), f32),
        in_specs=[anywhere] * 5,
        out_specs=pl.BlockSpec(memory_space=pltpu.VMEM),
        scratch_shapes=[
            pltpu.VMEM(query_hidden.shape, bf16),
            pltpu.VMEM(query_proj.shape, bf16),
            pltpu.VMEM(passages.shape, bf16),
            pltpu.VMEM(teacher.shape, f32),
            pltpu.VMEM((picks, qd), jnp.int32),
            pltpu.VMEM((mp, qd * share, emb), f32),
            pltpu.VMEM((mp, qd * share, emb), bf16),
            pltpu.VMEM((mp, qd * share, emb), bf16),
            pltpu.VMEM((2, own_p * pt, emb), bf16),
            pltpu.VMEM((dp, cap * share, qd * share), bf16),
            pltpu.VMEM((dp, 2, rows_b, emb), bf16),
            pltpu.VMEM((dp, mp, rows_b, emb), bf16),
            pltpu.VMEM((2 * own_p, mp * rows_b), f32),
            pltpu.VMEM((dp, half, 128), f32),
            pltpu.VMEM((dp, mp, half, 128), f32),
            pltpu.VMEM((dp * cap, teacher.shape[2]), f32),
            pltpu.VMEM((dp * cap, qd), f32),
            dma((5,)), dma((mp,)), dma((mp,)), dma, dma, dma((dp, mp)), dma((dp, mp)),
            dma((dp,)), dma((dp,)), dma((dp, mp)), dma((dp, mp)),
        ],
        compiler_params=pltpu.CompilerParams(
            collective_id=0, has_side_effects=True, vmem_limit_bytes=60 * 2**20
        ),
    )(query_hidden, query_proj, passages, teacher, neg_blocks.T)
    return loss.reshape(qd)


def soft_scores(slot_rows, passage_vecs):
    slot_count = slot_rows.shape[0]
    block_size = 16
    padded_count = -(-slot_count // block_size) * block_size
    blocked = slot_rows.reshape(
        padded_count // block_size, block_size, slot_rows.shape[1], slot_rows.shape[2]
    )

    def block_scores(slot_block):
        sims = jnp.einsum(
            "sie,pje->sipj", slot_block, passage_vecs, preferred_element_type=jnp.float32
        )
        softened = softness * jnp.log(jnp.sum(jnp.exp(sims / softness), axis=-1))
        return jnp.sum(softened, axis=1)

    scored = lax.map(block_scores, blocked)
    return scored.reshape(padded_count, -1)


def per_device(query_hidden, query_proj, passages, teacher, neg_blocks):
    partial_sum = jnp.einsum(
        "qth,he->qte", query_hidden, query_proj, preferred_element_type=jnp.float32
    )
    passage_vecs = unit_rows(passages.astype(jnp.float32)).astype(jnp.bfloat16)
    dp_count = lax.axis_size("dp")
    query_count, pick_count = neg_blocks.shape
    embed_width = partial_sum.shape[2]
    row_count = query_count * pick_count
    capacity = max(2, -(-row_count // dp_count))
    slots_all = dp_count * capacity
    owners = neg_blocks.reshape(row_count)
    owner_hits = (owners[:, None] == jnp.arange(dp_count, dtype=jnp.int32)[None, :]).astype(
        jnp.int32
    )
    order = jnp.arange(row_count, dtype=jnp.int32)
    before = (order[None, :] < order[:, None]).astype(jnp.float32)
    earlier = jnp.dot(
        before, owner_hits.astype(jnp.float32), preferred_element_type=jnp.float32
    ).astype(jnp.int32)
    slot_rank = jnp.sum(earlier * owner_hits, axis=1)
    slot_ids = owners * capacity + slot_rank
    matches = (slot_ids[None, :] == jnp.arange(slots_all, dtype=jnp.int32)[:, None]).astype(
        jnp.int32
    )
    chosen = jnp.sum(matches.reshape(slots_all, query_count, pick_count), axis=2)
    token_share = lax.psum_scatter(partial_sum, "mp", scatter_dimension=1, tiled=True)
    share_vecs = unit_rows(token_share).astype(jnp.bfloat16)
    quarter = share_vecs.shape[1]
    token_part = jnp.einsum(
        "sq,qte->ste", chosen.astype(jnp.bfloat16), share_vecs, preferred_element_type=jnp.float32
    ).astype(jnp.bfloat16)
    token_part = token_part.reshape(dp_count, capacity, quarter, embed_width)
    arrived = lax.all_to_all(token_part, "dp", split_axis=0, concat_axis=0, tiled=True)
    joined = lax.all_gather(arrived, "mp", axis=2, tiled=True)
    tokens = joined.shape[2]
    scores = soft_scores(joined.reshape(slots_all, tokens, embed_width), passage_vecs).reshape(
        dp_count, capacity, -1
    )
    returned = lax.all_to_all(scores, "dp", split_axis=0, concat_axis=0, tiled=True)
    home_scores = returned.reshape(slots_all, -1)[slot_ids].reshape(query_count, pick_count, -1)
    teacher_logp = teacher - jnp.log(jnp.sum(jnp.exp(teacher), axis=(1, 2), keepdims=True))
    student = lax.all_gather(home_scores, "mp", axis=2, tiled=True)
    kl_loss = jnp.sum(jnp.exp(teacher_logp) * (teacher_logp - student), axis=(1, 2)) + jnp.log(
        jnp.sum(jnp.exp(student), axis=(1, 2))
    )
    return kl_loss


def solution(mesh):
    in_specs = (
        P("dp", None, "mp"),
        P("mp", None),
        P(("dp", "mp"), None, None),
        P("dp", None, None),
        P("dp", None),
    )
    out_specs = P("dp")
    dp, mp = mesh.shape["dp"], mesh.shape["mp"]

    def whole(query_hidden, query_proj, passages, teacher, neg_blocks):
        qd, picks = neg_blocks.shape[0] // dp, neg_blocks.shape[1]
        cap = max(2, -(-(qd * picks) // dp))
        share = query_hidden.shape[1] // mp
        own_p = passages.shape[0] // (dp * mp)
        fits = (
            mp == 4 and dp & (dp - 1) == 0 and dp * mp <= 64 and share % 8 == 0
            and cap % 16 == 0 and cap <= 256 and own_p % 8 == 0 and own_p <= 64
        )
        return jax.shard_map(
            fused_device if fits else per_device, mesh=mesh, in_specs=in_specs,
            out_specs=out_specs, check_vma=False,
        )(query_hidden, query_proj, passages, teacher, neg_blocks)

    return whole
```
